32 devices in a mesh: grp: 2 (over y), exp: 4 (over z), dp: 2 (over x), tp: 2 (over core).
Axes of the slice: x: 2, y: 2, z: 4, core: 2. Of those that a mesh axis runs over, the one named last changes fastest.
Arguments:
- tokens: bfloat16 [1024, 7168], P(('grp', 'exp'), ('dp', 'tp')), parts along dimension 0, may hold values from -6 to 6
- cotangent: bfloat16 [1024, 7168], P(('grp', 'exp'), ('dp', 'tp')), parts along dimension 0, may hold values from -0.1796875 to 0.1796875
- expert_ids: int32 [1024, 2], P(('grp', 'exp')), parts along dimension 0, may hold values from 0 to 3, all different within a row; in each aligned block of 128 rows (0 to 127, 128 to 255, ...) at most 96 rows name the same one
- route_weights: bfloat16 [1024, 2], P(('grp', 'exp')), parts along dimension 0, may hold values from 0.049804688 to 0.59765625
- gate_weight: bfloat16 [8, 7168, 1024], P(('grp', 'exp'), ('dp', 'tp')), parts along dimension 0, may hold values from -0.0625 to 0.0625
- up_weight: bfloat16 [8, 7168, 1024], P(('grp', 'exp'), ('dp', 'tp')), parts along dimension 0, may hold values from -0.0625 to 0.0625
- down_weight: bfloat16 [8, 1024, 7168], P(('grp', 'exp'), None, ('dp', 'tp')), parts along dimension 0, may hold values from -0.1875 to 0.1875
- delta: bfloat16 [8, 1024, 7168], P(('grp', 'exp'), None, ('dp', 'tp')), parts along dimension 0, may hold values from -12 to 12
Outputs:
- grad_down: float32 [8, 1024, 7168], P(('grp', 'exp'), None, ('dp', 'tp')), parts along dimension 0
- unit_scores: float32 [8, 1024], P(('grp', 'exp'), ('dp', 'tp')), parts along dimension 0
- route_grads: float32 [1024, 2], P(('grp', 'exp')), parts along dimension 0
The draws below stay inside these ranges and needn't reach their ends.
There are 2 independent parts, one for each index of `grp`. The reference program is written for one: setup_inputs(seed, part) draws one part's arguments, and reference() takes and returns one part's arrays. A program takes and returns all parts, laid end to end along the dimension named above; each array names one. Nothing has to cross between parts.
Inputs may be any that keep to these rules, and one draw needn't show every extreme that they name: `expert_ids`: each token names 2 different experts. Within the 128 tokens of one index of exp no expert is named more than 96 times, and in every draw some expert is named exactly 96 times by the tokens of some index.
All inputs are finite; a program needn't handle non-finite values.
Results may differ from the reference program's by a relative error of at most 0.018.
Values may be sent and summed in bfloat16 or wider, within the bound.
A program may use at most 128 MiB of HBM per device.

```python
import math
import jax
import jax.numpy as jnp
import numpy as np
from jax import lax

D = 7168
FF = 1024
TOK_EXP = 128
EXPERTS = 4
TOP = 2
CAP = 96
ROWS = 384
BLOCKS = 4
DSLICE = 1792
TOKENS = 512
N_EXP = 4


def draw_delta(key, part):
    key = jax.random.fold_in(key, 7)
    first, second = jax.random.split(key)
    column = jnp.arange(D, dtype=jnp.float32) / D
    row_scale = jnp.exp(jax.random.uniform(second, (EXPERTS, FF, 1), jnp.float32, 0.0, math.log(10.0)))
    base = jnp.clip(jax.random.normal(first, (EXPERTS, FF, D), jnp.float32), -4.0, 4.0)
    ramp = jnp.power(10.0, column)
    return (0.02 * base * row_scale * ramp[None, None, :]).astype(jnp.bfloat16)


def block_scale(rng, shape, cuts, low, largest):
    level = 1.0
    for axis_at, shards_of in cuts:
        heights = jax.random.uniform(jax.random.fold_in(jax.random.fold_in(rng, 6), axis_at), (shards_of,), jnp.float32, low / len(cuts), largest / len(cuts))
        level = level * jnp.repeat(jnp.exp(heights), shape[axis_at] // shards_of).reshape((-1,) + (1,) * (len(shape) - 1 - axis_at))
    return level


def routed_block(stream_key, own, number, rows, amount, top, reach, slope):
    order = jax.random.permutation(stream_key, amount)
    heavy_load, ordinary = load_shares(amount, rows * top, reach, slope, True), load_shares(amount, rows * top, reach, slope, False)
    places = jnp.arange(amount)

    def named(lengths, turn):
        used = int((lengths > 0).sum())
        fixed = max(1, used // 4)
        shifted = fixed + (places - fixed + turn * (used - fixed)) % max(1, amount - fixed)
        return jnp.zeros((amount,), jnp.int32).at[order[jnp.where(places < fixed, places, shifted)]].set(jnp.asarray(lengths, jnp.int32))

    lengths = jnp.where(number % 4 == 0, named(heavy_load, number // 4), named(ordinary, number - number // 4 - 1))
    mixed = jax.random.permutation(jax.random.fold_in(own, 3), amount)
    giver, taker = mixed[0:amount // 2 * 2:2], mixed[1:amount // 2 * 2:2]
    room = jnp.minimum(lengths[giver] - 1, reach - lengths[taker]) // 2
    room = jnp.where((giver == order[0]) | (taker == order[0]) | (lengths[taker] == 0), 0, jnp.maximum(room, 0))
    shifted = jax.random.randint(jax.random.fold_in(own, 4), (amount // 2,), 0, 1 << 20) % (room + 1)
    lengths = lengths.at[giver].add(-shifted).at[taker].add(shifted)
    members = jnp.searchsorted(jnp.cumsum(lengths), jnp.arange(rows * top), side="right").astype(jnp.int32)
    grid = members.reshape(top, rows).T
    grid = grid[jax.random.permutation(jax.random.fold_in(own, 1), rows)]
    turn = jax.random.randint(jax.random.fold_in(own, 2), (rows, 1), 0, top)
    return jnp.take_along_axis(grid, (jnp.arange(top)[None, :] + turn) % top, axis=1)


def load_shares(count, total, bound, lean, full):
    loads = [(1 << 20) // math.isqrt(rank ** lean) + 1 for rank in range(1, count + 1)]
    largest = bound if full else min(bound, max(-(-total // count), total * loads[0] // sum(loads)))
    least = 1 if total - largest >= count - 1 else 0
    given, spare = [largest] + [least] * (count - 1), total - largest - least * (count - 1)
    while spare > 0:
        candidates = [i for i in range(1, count) if given[i] < largest] or [i for i in range(1, count) if given[i] < bound]
        mass, left = sum([loads[i] for i in candidates]), spare
        for i in candidates:
            extra = min(bound - given[i], max(1, left * loads[i] // mass), spare)
            given[i] = given[i] + extra
            spare = spare - extra
    return np.array(given)


def noise(stream_key, shape, scale, reach, cuts=(), kind=jnp.bfloat16):
    gain = block_scale(stream_key, shape, cuts, -0.22, 0.18) if cuts else 1.0
    values = jax.random.normal(stream_key, shape, jnp.float32) * scale * gain
    return jnp.minimum(jnp.maximum(values, -reach), reach).astype(kind)


def setup_inputs(seed: int = 0, part: int = 0) -> dict:
    key_of = jax.random.split(jax.random.key(seed), 9)
    part_keys = jax.random.split(jax.random.fold_in(key_of[8], part), 9)
    tokens = noise(part_keys[0], (TOKENS, D), 1.0, 6.0, ((0, 4), (1, 4)))
    cotangent = noise(part_keys[1], (TOKENS, D), 0.03, 0.1796875, ((0, 4), (1, 4)))
    expert_ids_keys = jax.random.split(jax.random.fold_in(part_keys[2], 1), TOKENS // TOK_EXP)
    expert_ids_turns = jax.random.permutation(jax.random.fold_in(part_keys[2], 3), TOKENS // TOK_EXP)
    expert_ids = jax.vmap(lambda own, number: routed_block(jax.random.fold_in(part_keys[2], 2), own, number, TOK_EXP, EXPERTS, TOP, CAP, 2))(expert_ids_keys, expert_ids_turns).reshape((TOKENS, TOP))
    route_weights = jnp.clip(0.049804688 + 0.54785156 * jax.random.uniform(part_keys[3], (TOKENS, TOP), jnp.float32) ** block_scale(part_keys[3], (TOKENS, TOP), ((0, 4),), -0.2, 0.2), 0.049804688, 0.59765625).astype(jnp.bfloat16)
    gate_weight = noise(part_keys[4], (EXPERTS, D, FF), D ** -0.5, 0.0625, ((0, 4), (1, 4)))
    up_weight = noise(part_keys[5], (EXPERTS, D, FF), D ** -0.5, 0.0625, ((0, 4), (1, 4)))
    down_weight = noise(part_keys[6], (EXPERTS, FF, D), FF ** -0.5, 0.1875, ((0, 4), (2, 4)))
    delta = draw_delta(jax.random.fold_in(jax.random.fold_in(key_of[8], part), 71), part)
    return {"tokens": tokens, "cotangent": cotangent, "expert_ids": expert_ids, "route_weights": route_weights, "gate_weight": gate_weight, "up_weight": up_weight, "down_weight": down_weight, "delta": delta}


def reference(tokens, cotangent, expert_ids, route_weights, gate_weight, up_weight, down_weight, delta):
    grouped = expert_ids.reshape(N_EXP, TOK_EXP * TOP)
    onehot = (grouped[:, :, None] == jnp.arange(EXPERTS, dtype=jnp.int32)[None, None, :]).astype(jnp.int32)
    earlier = jnp.cumsum(onehot, axis=1) - onehot
    slot = jnp.sum(earlier * onehot, axis=2).astype(jnp.int32)
    source = jnp.arange(N_EXP, dtype=jnp.int32)[:, None] * jnp.ones_like(slot)
    token_index = source * TOK_EXP + jnp.arange(TOK_EXP * TOP, dtype=jnp.int32)[None, :] // TOP
    place = (grouped * ROWS + source * CAP + slot).reshape(-1).astype(jnp.int32)
    table = jnp.full((EXPERTS * ROWS,), -1, jnp.int32).at[place].set(token_index.reshape(-1).astype(jnp.int32))
    weight_table = jnp.zeros((EXPERTS * ROWS,), jnp.float32).at[place].set(route_weights.reshape(-1).astype(jnp.float32))
    table = table.reshape(EXPERTS, ROWS)
    weight_table = weight_table.reshape(EXPERTS, ROWS)

    def expert_step(items):
        index, weight_rows, w_gate, w_up, w_down, change = items
        valid = (index >= 0)[:, None]
        safe = jnp.maximum(index, 0).astype(jnp.int32)
        rows = jnp.where(valid, tokens[safe].astype(jnp.float32), 0.0)
        cot_rows = jnp.where(valid, cotangent[safe].astype(jnp.float32), 0.0)
        split_rows = rows.reshape(ROWS, BLOCKS, DSLICE)

        def blocked(weight):
            parts = jnp.einsum("rbd,bdf->brf", split_rows, weight.astype(jnp.float32).reshape(BLOCKS, DSLICE, FF))
            parts = lax.optimization_barrier(parts.astype(jnp.bfloat16))
            return jnp.sum(parts.astype(jnp.float32), axis=0)

        gate = blocked(w_gate)
        upper = blocked(w_up)
        hidden = (jax.nn.silu(gate) * upper).astype(jnp.bfloat16)
        outputs = jnp.dot(hidden, w_down, preferred_element_type=jnp.float32)
        dots = jnp.sum(cot_rows * outputs, axis=1)
        upstream = (weight_rows[:, None] * cot_rows).astype(jnp.bfloat16)
        grad = jnp.dot(hidden.T, upstream, preferred_element_type=jnp.float32)
        score = jnp.log(jnp.mean((grad * change.astype(jnp.float32)) ** 2, axis=1) + 1e-6)
        return grad, score, dots

    grad_down, unit_scores, dots = lax.map(expert_step, (table, weight_table, gate_weight, up_weight, down_weight, delta))
    route_grads = dots.reshape(-1)[place].reshape(TOKENS, TOP)
    return grad_down, unit_scores, route_grads
```

```python
import functools

import jax
import jax.numpy as jnp
from jax import lax
from jax.experimental import pallas as pl
from jax.experimental.pallas import tpu as pltpu
from jax.sharding import PartitionSpec as P

MESH = pl.DeviceIdType.MESH
VMEM = pl.BlockSpec(memory_space=pltpu.VMEM)
HBM = pl.BlockSpec(memory_space=pl.ANY)
F32 = jnp.float32
BF16 = jnp.bfloat16


def remote(src, dst, send, recv, **where):
    return pltpu.make_async_remote_copy(
        src_ref=src, dst_ref=dst, send_sem=send, recv_sem=recv,
        device_id=where, device_id_type=MESH,
    )


def greet(n, ndp):
    me, d, t = lax.axis_index("exp"), lax.axis_index("dp"), lax.axis_index("tp")
    return me, d, t


def exchange_kernel(
    n, ndp, nc, cap,
    ids_ref, rw_ref, tok_ref, cot_ref, wg_hbm, wu_hbm,
    hid_ref, cpk_ref, ups_ref, pos_ref,
    wg, wu, meta, full, pk, pp, s1send, s1recv, s1own, s2send, s2recv, s2own, hb,
    wsem, ms, mr, fs, fr, ps, pr, s1s, s1r, s2s, s2r, hs, hr, ts, tr,
):
    me, d, t = lax.axis_index("exp"), lax.axis_index("dp"), lax.axis_index("tp")
    pairs = n // 2
    q, b = me // 2, me % 2
    mate = q * 2 + (1 - b)
    other = 1 - t
    rows, width = tok_ref.shape
    wc = width // nc
    ff = wg.shape[1]
    half = ff // 2
    part = half // ndp
    srcs = (tok_ref, cot_ref)
    group_rows = 2 * cap

    loads = [pltpu.make_async_copy(wg_hbm.at[0], wg, wsem.at[0]),
             pltpu.make_async_copy(wu_hbm.at[0], wu, wsem.at[1])]
    for load in loads:
        load.start()

    barrier = pltpu.get_barrier_semaphore()
    for i in range(1, n):
        pl.semaphore_signal(barrier, inc=1, device_id={"exp": lax.rem(me + i, n)}, device_id_type=MESH)
    for i in range(1, ndp):
        pl.semaphore_signal(barrier, inc=1, device_id={"dp": lax.rem(d + i, ndp)}, device_id_type=MESH)
    pl.semaphore_signal(barrier, inc=1, device_id={"tp": other}, device_id_type=MESH)

    ne = max(n, 16)
    expert = lax.broadcasted_iota(jnp.int32, (ne, rows), 0)
    named = jnp.zeros((ne, rows), F32)
    share = jnp.zeros((ne, rows), F32)
    for k in range(ids_ref.shape[0]):
        hit = expert == ids_ref[k:k + 1, :]
        named = named + jnp.where(hit, 1.0, 0.0)
        share = share + jnp.where(hit, rw_ref[k:k + 1, :], 0.0)
    before = (lax.broadcasted_iota(jnp.int32, (rows, rows), 0)
              < lax.broadcasted_iota(jnp.int32, (rows, rows), 1))
    count = jnp.dot(named.astype(BF16), jnp.where(before, 1.0, 0.0).astype(BF16),
                    preferred_element_type=F32)
    place = jnp.where(named > 0.5, count, -1.0)
    for e in range(n):
        meta[me, e, 0:1, :] = place[e:e + 1, :]
        meta[me, e, 1:2, :] = share[e:e + 1, :]
        meta[me, e, 2:8, :] = jnp.zeros((6, rows), F32)

    pl.semaphore_wait(barrier, n - 1 + ndp)

    slot_iota = lax.broadcasted_iota(jnp.int32, (cap, rows), 0).astype(F32)

    def placing(s, e):
        return jnp.where(meta[s, e, 0:1, :] == slot_iota, 1.0, 0.0).astype(BF16)

    def cols(c):
        return slice(c * wc, (c + 1) * wc)

    def meta_copy(to):
        pair = pl.ds(2 * (to // 2), 2)
        return remote(meta.at[me, pair], meta.at[me, pair], ms.at[to], mr.at[me], exp=to)

    def meta_arrive(s):
        pair = pl.ds(2 * q, 2)
        return remote(meta.at[s, pair], meta.at[s, pair], ms.at[s], mr.at[s], exp=s)

    def full_copy(a, p, c):
        to = 2 * p + jnp.where(p > q, 0, 1)
        return remote(srcs[a].at[:, cols(c)], full.at[a, me, :, cols(c)],
                      fs.at[a, p, c], fr.at[a, me, c], exp=to)

    def full_arrive(a, s, c):
        return remote(srcs[a].at[:, cols(c)], full.at[a, s, :, cols(c)],
                      fs.at[a, q, c], fr.at[a, s, c], exp=mate)

    def pack_copy(a, s, c):
        return remote(pp.at[a, s, :, cols(c)], pk.at[a, s, :, cols(c)],
                      ps.at[a, s, c], pr.at[a, s, c], exp=mate)

    def own_sends(a):
        for c in range(nc):
            for g in range(1, pairs):
                full_copy(a, lax.rem(q + g, pairs), c).start()
        to_mate = placing(me, mate)
        for c in range(nc):
            pp[a, me, :, cols(c)] = jnp.dot(
                to_mate, srcs[a][:, cols(c)], preferred_element_type=F32).astype(BF16)
            pack_copy(a, me, c).start()
        mine = placing(me, me)
        for c in range(nc):
            pk[a, me, :, cols(c)] = jnp.dot(
                mine, srcs[a][:, cols(c)], preferred_element_type=F32).astype(BF16)

    def own_sent(a):
        for g in range(1, pairs):
            for c in range(nc):
                full_copy(a, lax.rem(q + g, pairs), c).wait_send()
        for c in range(nc):
            pack_copy(a, me, c).wait_send()

    def is_near(p):
        return ((p < q) & (b == 0)) | ((p > q) & (b == 1))

    def relay(a, g, c):
        p = lax.rem(q + g, pairs)

        @pl.when(is_near(p))
        def _():
            for j in range(2):
                s = 2 * p + j
                full_arrive(a, s, c).wait_recv()
                block = full[a, s, :, cols(c)]
                pp[a, s, :, cols(c)] = jnp.dot(
                    placing(s, mate), block, preferred_element_type=F32).astype(BF16)
                pack_copy(a, s, c).start()
                pk[a, s, :, cols(c)] = jnp.dot(
                    placing(s, me), block, preferred_element_type=F32).astype(BF16)

    def arrived(a, g):
        p = lax.rem(q + g, pairs)
        if g == 0:
            for c in range(nc):
                pack_copy(a, mate, c).wait_recv()
        else:
            @pl.when(jnp.logical_not(is_near(p)))
            def _():
                for j in range(2):
                    for c in range(nc):
                        pack_copy(a, 2 * p + j, c).wait_recv()

    def s1_copy(g):
        return remote(s1send.at[g], s1recv.at[g], s1s.at[g], s1r.at[g], tp=other)

    def s2_copy(g, to):
        return remote(s2send.at[g, to], s2recv.at[g, d], s2s.at[g, to], s2r.at[g, d], dp=to)

    def s2_arrive(g, frm):
        return remote(s2send.at[g, frm], s2recv.at[g, frm], s2s.at[g, frm], s2r.at[g, frm], dp=frm)

    def h_copy(g, to):
        return remote(hb.at[g, t, d], hb.at[g, t, d], hs.at[g, to], hr.at[g, d], dp=to)

    def h_arrive(g, frm):
        return remote(hb.at[g, t, frm], hb.at[g, t, frm], hs.at[g, frm], hr.at[g, frm], dp=frm)

    def t_copy(g, i):
        return remote(hb.at[g, t, i], hb.at[g, t, i], ts.at[g, i], tr.at[g, i], tp=other)

    def t_arrive(g, i):
        return remote(hb.at[g, other, i], hb.at[g, other, i], ts.at[g, i], tr.at[g, i], tp=other)

    tile = min(256, half)

    def products(g):
        p = lax.rem(q + g, pairs)

        def into(target, side):
            @pl.loop(0, half // tile)
            def _(i):
                x = pk[0, pl.ds(2 * p, 2)].reshape(group_rows, width)
                at = pl.ds(pl.multiple_of(side * half + i * tile, tile), tile)
                put = pl.ds(pl.multiple_of(i * tile, tile), tile)
                target[g, 0, :, put] = jnp.dot(x, wg[:, at], preferred_element_type=F32).astype(BF16)
                target[g, 1, :, put] = jnp.dot(x, wu[:, at], preferred_element_type=F32).astype(BF16)

        into(s1send, other)
        s1_copy(g).start()
        into(s1own, t)

    def sums(g):
        s1_copy(g).wait_recv()
        for i in range(ndp):
            at = slice(i * part, (i + 1) * part)
            total = s1own[g, :, :, at].astype(F32) + s1recv[g, :, :, at].astype(F32)
            s2send[g, i] = total.astype(BF16)

            @pl.when(d == i)
            def _():
                s2own[g] = total
        for i in range(1, ndp):
            s2_copy(g, lax.rem(d + i, ndp)).start()

    def activate(g):
        total = s2own[g]
        for i in range(1, ndp):
            frm = lax.rem(d + i, ndp)
            s2_arrive(g, frm).wait_recv()
            total = total + s2recv[g, frm].astype(F32)
        gate, upper = total[0], total[1]
        hb[g, t, d] = (gate / (1.0 + jnp.exp(-gate)) * upper).astype(BF16)
        for i in range(1, ndp):
            h_copy(g, lax.rem(d + i, ndp)).start()
        t_copy(g, d).start()

    def forward(g):
        for i in range(1, ndp):
            frm = lax.rem(d + i, ndp)
            h_arrive(g, frm).wait_recv()
            t_copy(g, frm).start()

    def finish(g):
        p = lax.rem(q + g, pairs)
        for i in range(ndp):
            t_arrive(g, i).wait_recv()
        for side in range(2):
            for i in range(ndp):
                at = side * half + i * part
                hid_ref[p, :, at:at + part] = hb[g, side, i]

    def upstream(g):
        p = lax.rem(q + g, pairs)
        for j in range(2):
            s = 2 * p + j
            spread = jnp.where(meta[s, me, 0:1, :] == slot_iota, meta[s, me, 1:2, :], 0.0)
            scale = jnp.sum(spread, axis=1, keepdims=True)
            block = pk[1, s]
            cpk_ref[s] = block
            ups_ref[s] = (scale * block.astype(F32)).astype(BF16)

    for i in range(1, n):
        meta_copy(lax.rem(me + i, n)).start()
    own_sends(0)
    for i in range(1, n):
        meta_arrive(lax.rem(me + i, n)).wait_recv()
    for s in range(n):
        pos_ref[s] = meta[s, me, 0:1, :]

    for g in range(1, pairs):
        for c in range(nc - 1):
            relay(0, g, c)
    for load in loads:
        load.wait()
    arrived(0, 0)
    products(0)
    sums(0)
    for g in range(1, pairs):
        relay(0, g, nc - 1)
    own_sent(0)
    own_sends(1)
    activate(0)
    forward(0)
    for g in range(1, pairs):
        arrived(0, g)
        products(g)
        sums(g)
    finish(0)
    for g in range(1, pairs):
        for c in range(nc - 1):
            relay(1, g, c)
    for g in range(1, pairs):
        activate(g)
    for g in range(1, pairs):
        forward(g)
    for g in range(1, pairs):
        finish(g)
    arrived(1, 0)
    upstream(0)
    for g in range(1, pairs):
        relay(1, g, nc - 1)
    for g in range(1, pairs):
        arrived(1, g)
        upstream(g)

    for i in range(1, n):
        meta_copy(lax.rem(me + i, n)).wait_send()
    own_sent(1)
    for g in range(pairs):
        s1_copy(g).wait_send()
        for i in range(1, ndp):
            s2_copy(g, lax.rem(d + i, ndp)).wait_send()
            h_copy(g, lax.rem(d + i, ndp)).wait_send()
        for i in range(ndp):
            t_copy(g, i).wait_send()
        if g:
            p = lax.rem(q + g, pairs)

            @pl.when(is_near(p))
            def _():
                for a in range(2):
                    for j in range(2):
                        for c in range(nc):
                            pack_copy(a, 2 * p + j, c).wait_send()


def gradient_kernel(n, cap, tile, hid_ref, ups_ref, cpk_ref, pos_ref, wd_ref, delta_ref,
                    grad_ref, stat_ref, dots):
    step = pl.program_id(0)
    h = hid_ref[...]
    grad = lax.dot_general(h, ups_ref[...], (((0,), (0,)), ((), ())), preferred_element_type=F32)
    grad_ref[0] = grad
    term = grad * delta_ref[0].astype(F32)
    term = term * term
    lanes = term[:, 0:128]
    for i in range(1, term.shape[1] // 128):
        lanes = lanes + term[:, i * 128:(i + 1) * 128]
    for i in range(tile // 128):
        stat_ref[n + step * (tile // 128) + i] = jnp.sum(
            lanes[i * 128:(i + 1) * 128, :].T, axis=0, keepdims=True)
    back = lax.dot_general(cpk_ref[...], wd_ref[0], (((1,), (1,)), ((), ())), preferred_element_type=F32)
    inner = jnp.sum(back * h.astype(F32), axis=1, keepdims=True)

    @pl.when(step == 0)
    def _():
        dots[...] = inner

    @pl.when(step > 0)
    def _():
        dots[...] += inner

    @pl.when(step == pl.num_programs(0) - 1)
    def _():
        slot = lax.broadcasted_iota(jnp.int32, (cap, 128), 0).astype(F32)
        for s in range(n):
            mine = jnp.where(pos_ref[s] == slot, dots[s * cap:(s + 1) * cap, :], 0.0)
            stat_ref[s] = jnp.sum(mine, axis=0, keepdims=True)


def reduce_kernel(n, ndp, features, stat_ref, ids_ref, unit_ref, route_ref,
                  got, total, back, gs, gr, bs, br):
    me, d, t = lax.axis_index("exp"), lax.axis_index("dp"), lax.axis_index("tp")
    own = d * 2 + t
    peers = 2 * ndp
    barrier = pltpu.get_barrier_semaphore()

    def peer(i):
        to = lax.rem(own + i, peers)
        return to, {"dp": to // 2, "tp": lax.rem(to, 2)}

    for i in range(1, peers):
        pl.semaphore_signal(barrier, inc=1, device_id=peer(i)[1], device_id_type=MESH)
    for i in range(1, n):
        pl.semaphore_signal(barrier, inc=1, device_id={"exp": lax.rem(me + i, n)}, device_id_type=MESH)
    pl.semaphore_wait(barrier, peers - 1 + n - 1)

    def gather(i):
        to, where = peer(i)
        return remote(stat_ref, got.at[own], gs.at[to], gr.at[own], **where)

    def gathered(i):
        frm, where = peer(i)
        return remote(stat_ref, got.at[frm], gs.at[frm], gr.at[frm], **where)

    for i in range(1, peers):
        gather(i).start()
    got[own] = stat_ref[...]
    for i in range(1, peers):
        gathered(i).wait_recv()
    added = got[0]
    for i in range(1, peers):
        added = added + got[i]
    total[...] = added

    def give(to):
        return remote(total.at[to], back.at[me], bs.at[to], br.at[me], exp=to)

    def given(frm):
        return remote(total.at[frm], back.at[frm], bs.at[frm], br.at[frm], exp=frm)

    for i in range(1, n):
        give(lax.rem(me + i, n)).start()
    back[me] = total[me]
    units = unit_ref.shape[0]
    unit_ref[...] = jnp.log(total[pl.ds(n + own * units, units)] / features + 1e-6)
    for i in range(1, n):
        given(lax.rem(me + i, n)).wait_recv()
    for k in range(ids_ref.shape[0]):
        chosen = ids_ref[k:k + 1, :]
        picked = jnp.zeros(chosen.shape, F32)
        for e in range(n):
            picked = picked + jnp.where(chosen == e, back[e], 0.0)
        route_ref[k:k + 1, :] = picked
    for i in range(1, peers):
        gather(i).wait_send()
    for i in range(1, n):
        give(lax.rem(me + i, n)).wait_send()


def shards(tokens, cotangent, expert_ids, route_weights, gate_weight, up_weight, down_weight, delta):
    n, ndp = lax.axis_size("exp"), lax.axis_size("dp")
    rows, width = tokens.shape
    chosen = expert_ids.shape[1]
    cap = rows * chosen * 3 // (2 * n)
    total = n * cap
    ff = gate_weight.shape[2]
    half, pairs = ff // 2, n // 2
    part = half // ndp
    nc = 2 if width % 256 == 0 else 1
    ids = expert_ids.T
    shares = route_weights.T.astype(F32)
    dma = pltpu.SemaphoreType.DMA
    hidden, cpk, ups, pos = pl.pallas_call(
        functools.partial(exchange_kernel, n, ndp, nc, cap),
        out_shape=(
            jax.ShapeDtypeStruct((pairs, 2 * cap, ff), BF16),
            jax.ShapeDtypeStruct((n, cap, width), BF16),
            jax.ShapeDtypeStruct((n, cap, width), BF16),
            jax.ShapeDtypeStruct((n, 1, rows), F32),
        ),
        in_specs=[VMEM, VMEM, VMEM, VMEM, HBM, HBM],
        out_specs=(VMEM, VMEM, VMEM, VMEM),
        scratch_shapes=[
            pltpu.VMEM((width, ff), BF16),
            pltpu.VMEM((width, ff), BF16),
            pltpu.VMEM((n, n, 8, rows), F32),
            pltpu.VMEM((2, n, rows, width), BF16),
            pltpu.VMEM((2, n, cap, width), BF16),
            pltpu.VMEM((2, n, cap, width), BF16),
            pltpu.VMEM((pairs, 2, 2 * cap, half), BF16),
            pltpu.VMEM((pairs, 2, 2 * cap, half), BF16),
            pltpu.VMEM((pairs, 2, 2 * cap, half), BF16),
            pltpu.VMEM((pairs, ndp, 2, 2 * cap, part), BF16),
            pltpu.VMEM((pairs, ndp, 2, 2 * cap, part), BF16),
            pltpu.VMEM((pairs, 2, 2 * cap, part), F32),
            pltpu.VMEM((pairs, 2, ndp, 2 * cap, part), BF16),
            dma((2,)), dma((n,)), dma((n,)),
            dma((2, pairs, nc)), dma((2, n, nc)), dma((2, n, nc)), dma((2, n, nc)),
            dma((pairs,)), dma((pairs,)),
            dma((pairs, ndp)), dma((pairs, ndp)),
            dma((pairs, ndp)), dma((pairs, ndp)),
            dma((pairs, ndp)), dma((pairs, ndp)),
        ],
        compiler_params=pltpu.CompilerParams(
            collective_id=0, has_side_effects=True, vmem_limit_bytes=60 * 2**20),
        name="exchange",
    )(ids, shares, tokens, cotangent, gate_weight, up_weight)

    tile = 256
    stats = n + ff // 128
    whole = lambda shape: pl.BlockSpec(shape, lambda i: (0,) * len(shape))
    grad, stat = pl.pallas_call(
        functools.partial(gradient_kernel, n, cap, tile),
        grid=(ff // tile,),
        out_shape=(
            jax.ShapeDtypeStruct((1, ff, width), F32),
            jax.ShapeDtypeStruct((stats, 1, 128), F32),
        ),
        in_specs=[
            pl.BlockSpec((total, tile), lambda i: (0, i)),
            whole((total, width)),
            whole((total, width)),
            whole((n, 1, rows)),
            pl.BlockSpec((1, tile, width), lambda i: (0, i, 0)),
            pl.BlockSpec((1, tile, width), lambda i: (0, i, 0)),
        ],
        out_specs=(
            pl.BlockSpec((1, tile, width), lambda i: (0, i, 0)),
            whole((stats, 1, 128)),
        ),
        scratch_shapes=[pltpu.VMEM((total, 1), F32)],
        compiler_params=pltpu.CompilerParams(vmem_limit_bytes=56 * 2**20),
        name="gradient",
    )(hidden.reshape(total, ff), ups.reshape(total, width), cpk.reshape(total, width),
      pos, down_weight, delta)

    units = ff // (2 * ndp) // 128
    unit, route = pl.pallas_call(
        functools.partial(reduce_kernel, n, ndp, float(width * 2 * ndp)),
        out_shape=(
            jax.ShapeDtypeStruct((units, 1, 128), F32),
            jax.ShapeDtypeStruct((chosen, rows), F32),
        ),
        in_specs=[VMEM, VMEM],
        out_specs=(VMEM, VMEM),
        scratch_shapes=[
            pltpu.VMEM((2 * ndp, stats, 1, 128), F32),
            pltpu.VMEM((stats, 1, 128), F32),
            pltpu.VMEM((n, 1, 128), F32),
            dma((2 * ndp,)), dma((2 * ndp,)), dma((n,)), dma((n,)),
        ],
        compiler_params=pltpu.CompilerParams(collective_id=1, has_side_effects=True),
        name="reduce",
    )(stat, ids)
    return grad, unit.reshape(1, units * 128), route.T


def solution(mesh):
    return jax.shard_map(
        shards,
        mesh=mesh,
        in_specs=(
            P(("grp", "exp"), ("dp", "tp")),
            P(("grp", "exp"), ("dp", "tp")),
            P(("grp", "exp"), None),
            P(("grp", "exp"), None),
            P(("grp", "exp"), ("dp", "tp"), None),
            P(("grp", "exp"), ("dp", "tp"), None),
            P(("grp", "exp"), None, ("dp", "tp")),
            P(("grp", "exp"), None, ("dp", "tp")),
        ),
        out_specs=(
            P(("grp", "exp"), None, ("dp", "tp")),
            P(("grp", "exp"), ("dp", "tp")),
            P(("grp", "exp"), None),
        ),
        check_vma=False,
    )
```

```python
import functools

import jax
import jax.numpy as jnp
from jax import lax
from jax.experimental import pallas as pl
from jax.experimental.pallas import tpu as pltpu
from jax.sharding import PartitionSpec as P

MESH = pl.DeviceIdType.MESH
VMEM = pl.BlockSpec(memory_space=pltpu.VMEM)
HBM = pl.BlockSpec(memory_space=pl.ANY)
F32 = jnp.float32
BF16 = jnp.bfloat16


def remote(src, dst, send, recv, **where):
    return pltpu.make_async_remote_copy(
        src_ref=src, dst_ref=dst, send_sem=send, recv_sem=recv,
        device_id=where, device_id_type=MESH,
    )


def exchange_kernel(
    n, ndp, edges, cap,
    ids_ref, rw_ref, tok_ref, cot_ref, wg_hbm, wu_hbm, wd_hbm,
    hid_ref, ups_ref, dots_ref,
    wg, wu, wd, meta, full, pk, pp, s1send, s1recv, s1own, s2send, s2recv, s2own, hb,
    wsem, ms, mr, fs, fr, ps, pr, s1s, s1r, s2s, s2r, hs, hr, ts, tr,
):
    me, d, t = lax.axis_index("exp"), lax.axis_index("dp"), lax.axis_index("tp")
    pairs = n // 2
    q, b = me // 2, me % 2
    mate = q * 2 + (1 - b)
    other = 1 - t
    rows, width = tok_ref.shape
    nc = len(edges) - 1
    ff = wg.shape[1]
    half = ff // 2
    part = half // ndp
    srcs = (tok_ref, cot_ref)
    group_rows = 2 * cap

    loads = [pltpu.make_async_copy(wg_hbm.at[0], wg, wsem.at[0]),
             pltpu.make_async_copy(wu_hbm.at[0], wu, wsem.at[1]),
             pltpu.make_async_copy(wd_hbm.at[0], wd, wsem.at[2])]
    for load in loads:
        load.start()

    barrier = pltpu.get_barrier_semaphore()
    for i in range(1, n):
        pl.semaphore_signal(barrier, inc=1, device_id={"exp": lax.rem(me + i, n)}, device_id_type=MESH)
    for i in range(1, ndp):
        pl.semaphore_signal(barrier, inc=1, device_id={"dp": lax.rem(d + i, ndp)}, device_id_type=MESH)
    pl.semaphore_signal(barrier, inc=1, device_id={"tp": other}, device_id_type=MESH)

    ne = max(n, 16)
    expert = lax.broadcasted_iota(jnp.int32, (ne, rows), 0)
    named = jnp.zeros((ne, rows), F32)
    share = jnp.zeros((ne, rows), F32)
    for k in range(ids_ref.shape[0]):
        hit = expert == ids_ref[k:k + 1, :]
        named = named + jnp.where(hit, 1.0, 0.0)
        share = share + jnp.where(hit, rw_ref[k:k + 1, :].astype(F32), 0.0)
    before = (lax.broadcasted_iota(jnp.int32, (rows, rows), 0)
              < lax.broadcasted_iota(jnp.int32, (rows, rows), 1))
    count = jnp.dot(named.astype(BF16), jnp.where(before, 1.0, 0.0).astype(BF16),
                    preferred_element_type=F32)
    place = jnp.where(named > 0.5, count, -1.0)
    for e in range(n):
        meta[me, e, 0:1, :] = place[e:e + 1, :]
        meta[me, e, 1:2, :] = share[e:e + 1, :]
        meta[me, e, 2:8, :] = jnp.zeros((6, rows), F32)

    pl.semaphore_wait(barrier, n - 1 + ndp)

    slot_iota = lax.broadcasted_iota(jnp.int32, (cap, rows), 0).astype(F32)

    def placing(s, e):
        return jnp.where(meta[s, e, 0:1, :] == slot_iota, 1.0, 0.0).astype(BF16)

    def cols(c):
        return slice(edges[c], edges[c + 1])

    def meta_copy(to):
        pair = pl.ds(2 * (to // 2), 2)
        return remote(meta.at[me, pair], meta.at[me, pair], ms.at[to], mr.at[me], exp=to)

    def meta_arrive(s):
        pair = pl.ds(2 * q, 2)
        return remote(meta.at[s, pair], meta.at[s, pair], ms.at[s], mr.at[s], exp=s)

    def full_copy(a, p, c):
        to = 2 * p + jnp.where(p > q, 0, 1)
        return remote(srcs[a].at[:, cols(c)], full.at[a, me, :, cols(c)],
                      fs.at[a, p, c], fr.at[a, me, c], exp=to)

    def full_arrive(a, s, c):
        return remote(srcs[a].at[:, cols(c)], full.at[a, s, :, cols(c)],
                      fs.at[a, q, c], fr.at[a, s, c], exp=mate)

    def pack_copy(a, s, c):
        return remote(pp.at[a, s, :, cols(c)], pk.at[a, s, :, cols(c)],
                      ps.at[a, s, c], pr.at[a, s, c], exp=mate)

    def placing_both(s):
        return jnp.concatenate([placing(s, mate), placing(s, me)], axis=0)

    def pack(a, s, c, both, block):
        packed = jnp.dot(both, block, preferred_element_type=F32).astype(BF16)
        pp[a, s, :, cols(c)] = packed[:cap]
        pack_copy(a, s, c).start()
        pk[a, s, :, cols(c)] = packed[cap:]

    def own_sends(a):
        for c in range(nc):
            for g in range(1, pairs):
                full_copy(a, lax.rem(q + g, pairs), c).start()
        both = placing_both(me)
        for c in range(nc):
            pack(a, me, c, both, srcs[a][:, cols(c)])

    def own_sent(a):
        for g in range(1, pairs):
            for c in range(nc):
                full_copy(a, lax.rem(q + g, pairs), c).wait_send()
        for c in range(nc):
            pack_copy(a, me, c).wait_send()

    def is_near(p):
        return ((p < q) & (b == 0)) | ((p > q) & (b == 1))

    def relay(a, g, c):
        p = lax.rem(q + g, pairs)

        @pl.when(is_near(p))
        def _():
            for j in range(2):
                s = 2 * p + j
                full_arrive(a, s, c).wait_recv()
                pack(a, s, c, placing_both(s), full[a, s, :, cols(c)])

    def arrived(a, g):
        p = lax.rem(q + g, pairs)
        if g == 0:
            for c in range(nc):
                pack_copy(a, mate, c).wait_recv()
        else:
            @pl.when(jnp.logical_not(is_near(p)))
            def _():
                for j in range(2):
                    for c in range(nc):
                        pack_copy(a, 2 * p + j, c).wait_recv()

    def s1_copy(g):
        return remote(s1send.at[g], s1recv.at[g], s1s.at[g], s1r.at[g], tp=other)

    def s2_copy(g, to):
        return remote(s2send.at[g, to], s2recv.at[g, d], s2s.at[g, to], s2r.at[g, d], dp=to)

    def s2_arrive(g, frm):
        return remote(s2send.at[g, frm], s2recv.at[g, frm], s2s.at[g, frm], s2r.at[g, frm], dp=frm)

    def h_copy(g, to):
        return remote(hb.at[g, t, d], hb.at[g, t, d], hs.at[g, to], hr.at[g, d], dp=to)

    def h_arrive(g, frm):
        return remote(hb.at[g, t, frm], hb.at[g, t, frm], hs.at[g, frm], hr.at[g, frm], dp=frm)

    def t_copy(g, i):
        return remote(hb.at[g, t, i], hb.at[g, t, i], ts.at[g, i], tr.at[g, i], tp=other)

    def t_arrive(g, i):
        return remote(hb.at[g, other, i], hb.at[g, other, i], ts.at[g, i], tr.at[g, i], tp=other)

    tile = min(256, half)

    def products(g):
        p = lax.rem(q + g, pairs)

        def into(target, side):
            @pl.loop(0, half // tile)
            def _(i):
                x = pk[0, pl.ds(2 * p, 2)].reshape(group_rows, width)
                at = pl.ds(pl.multiple_of(side * half + i * tile, tile), tile)
                put = pl.ds(pl.multiple_of(i * tile, tile), tile)
                target[g, 0, :, put] = jnp.dot(x, wg[:, at], preferred_element_type=F32).astype(BF16)
                target[g, 1, :, put] = jnp.dot(x, wu[:, at], preferred_element_type=F32).astype(BF16)

        into(s1send, other)
        s1_copy(g).start()
        into(s1own, t)

    def sums(g):
        s1_copy(g).wait_recv()
        for i in range(ndp):
            at = slice(i * part, (i + 1) * part)
            total = s1own[g, :, :, at].astype(F32) + s1recv[g, :, :, at].astype(F32)
            s2send[g, i] = total.astype(BF16)

            @pl.when(d == i)
            def _():
                s2own[g] = total
        for i in range(1, ndp):
            s2_copy(g, lax.rem(d + i, ndp)).start()

    def activate(g):
        total = s2own[g]
        for i in range(1, ndp):
            frm = lax.rem(d + i, ndp)
            s2_arrive(g, frm).wait_recv()
            total = total + s2recv[g, frm].astype(F32)
        gate, upper = total[0], total[1]
        hb[g, t, d] = (gate / (1.0 + jnp.exp(-gate)) * upper).astype(BF16)
        for i in range(1, ndp):
            h_copy(g, lax.rem(d + i, ndp)).start()
        t_copy(g, d).start()

    def forward(g):
        for i in range(1, ndp):
            frm = lax.rem(d + i, ndp)
            h_arrive(g, frm).wait_recv()
            t_copy(g, frm).start()

    def finish(g):
        p = lax.rem(q + g, pairs)
        for i in range(ndp):
            t_arrive(g, i).wait_recv()
        for side in range(2):
            for i in range(ndp):
                at = side * half + i * part
                hid_ref[p, :, at:at + part] = hb[g, side, i]

    def upstream(g):
        p = lax.rem(q + g, pairs)
        step = min(256, ff)

        def inner(i, acc):
            at = pl.ds(pl.multiple_of(i * step, step), step)
            x = pk[1, pl.ds(2 * p, 2)].reshape(group_rows, width)
            back = lax.dot_general(x, wd[at, :], (((1,), (1,)), ((), ())), preferred_element_type=F32)
            return acc + jnp.sum(back * hid_ref[p, :, at].astype(F32), axis=1, keepdims=True)

        dots = lax.fori_loop(0, ff // step, inner, jnp.zeros((group_rows, 1), F32))
        for j in range(2):
            s = 2 * p + j
            hit = meta[s, me, 0:1, :] == slot_iota
            scale = jnp.sum(jnp.where(hit, meta[s, me, 1:2, :], 0.0), axis=1, keepdims=True)
            ups_ref[s] = (scale * pk[1, s].astype(F32)).astype(BF16)
            dots_ref[s] = jnp.sum(
                jnp.where(hit, dots[j * cap:(j + 1) * cap], 0.0), axis=0, keepdims=True)

    for i in range(1, n):
        meta_copy(lax.rem(me + i, n)).start()
    own_sends(0)
    own_sends(1)
    for i in range(1, n):
        meta_arrive(lax.rem(me + i, n)).wait_recv()

    others = range(1, pairs)
    for g in others:
        for c in range(nc - 1):
            relay(0, g, c)
    for load in loads[:2]:
        load.wait()
    arrived(0, 0)
    products(0)
    for g in others:
        relay(0, g, nc - 1)
    sums(0)
    activate(0)
    for g in others:
        arrived(0, g)
        products(g)
        if g == 1:
            forward(0)
        sums(g)
    for g in others:
        relay(1, g, 0)
    finish(0)
    for g in others:
        activate(g)
    for g in others:
        if nc > 2:
            relay(1, g, 1)
    for g in others:
        forward(g)
    for g in others:
        for c in range(2, nc - 1):
            relay(1, g, c)
    for g in others:
        finish(g)
    loads[2].wait()
    arrived(1, 0)
    upstream(0)
    for g in others:
        if nc > 1:
            relay(1, g, nc - 1)
    for g in others:
        arrived(1, g)
        upstream(g)

    for i in range(1, n):
        meta_copy(lax.rem(me + i, n)).wait_send()
    own_sent(0)
    own_sent(1)
    for g in range(pairs):
        s1_copy(g).wait_send()
        for i in range(1, ndp):
            s2_copy(g, lax.rem(d + i, ndp)).wait_send()
            h_copy(g, lax.rem(d + i, ndp)).wait_send()
        for i in range(ndp):
            t_copy(g, i).wait_send()
        if g:
            p = lax.rem(q + g, pairs)

            @pl.when(is_near(p))
            def _():
                for a in range(2):
                    for j in range(2):
                        for c in range(nc):
                            pack_copy(a, 2 * p + j, c).wait_send()


def gradient_kernel(tile, hid_ref, ups_ref, delta_ref, grad_ref, sal_ref):
    grad = lax.dot_general(hid_ref[...], ups_ref[...], (((0,), (0,)), ((), ())),
                           preferred_element_type=F32)
    grad_ref[0] = grad
    term = grad * delta_ref[0].astype(F32)
    term = term * term
    lanes = term[:, 0:128]
    for i in range(1, term.shape[1] // 128):
        lanes = lanes + term[:, i * 128:(i + 1) * 128]
    for i in range(tile // 128):
        sal_ref[i] = jnp.sum(lanes[i * 128:(i + 1) * 128, :].T, axis=0, keepdims=True)


def reduce_kernel(n, ndp, features, dots_ref, sal_ref, ids_ref, unit_ref, route_ref,
                  got, sums, rs, rr, ss, sr):
    me, d, t = lax.axis_index("exp"), lax.axis_index("dp"), lax.axis_index("tp")
    own = d * 2 + t
    peers = 2 * ndp
    units = unit_ref.shape[0]
    barrier = pltpu.get_barrier_semaphore()
    hops = [(i, j) for i in range(n) for j in range(peers) if i or j]

    def there(i, j):
        e, o = lax.rem(me + i, n), lax.rem(own + j, peers)
        return e, o, {"exp": e, "dp": o // 2, "tp": lax.rem(o, 2)}

    for i, j in hops:
        pl.semaphore_signal(barrier, inc=1, device_id=there(i, j)[2], device_id_type=MESH)
    pl.semaphore_wait(barrier, len(hops))

    def slice_copy(j):
        e, o, where = there(0, j)
        return remote(sal_ref.at[pl.ds(o * units, units)], sums.at[own], ss.at[o], sr.at[own], **where)

    def slice_arrive(j):
        e, o, where = there(0, j)
        return remote(sal_ref.at[pl.ds(o * units, units)], sums.at[o], ss.at[o], sr.at[o], **where)

    def row_copy(i, j):
        e, o, where = there(i, j)
        return remote(dots_ref.at[e], got.at[me, own], rs.at[e, o], rr.at[me, own], **where)

    def row_arrive(i, j):
        e, o, where = there(i, j)
        return remote(dots_ref.at[e], got.at[e, o], rs.at[e, o], rr.at[e, o], **where)

    for j in range(1, peers):
        slice_copy(j).start()
    for i, j in hops:
        row_copy(i, j).start()
    sums[own] = sal_ref[pl.ds(own * units, units)]
    got[me, own] = dots_ref[me]
    for j in range(1, peers):
        slice_arrive(j).wait_recv()
    total = sums[0]
    for j in range(1, peers):
        total = total + sums[j]
    unit_ref[...] = jnp.log(total / features + 1e-6)
    for i, j in hops:
        row_arrive(i, j).wait_recv()
    rows = []
    for e in range(n):
        row = got[e, 0]
        for j in range(1, peers):
            row = row + got[e, j]
        rows.append(row)
    for k in range(ids_ref.shape[0]):
        chosen = ids_ref[k:k + 1, :]
        picked = jnp.zeros(chosen.shape, F32)
        for e in range(n):
            picked = picked + jnp.where(chosen == e, rows[e], 0.0)
        route_ref[k:k + 1, :] = picked
    for j in range(1, peers):
        slice_copy(j).wait_send()
    for i, j in hops:
        row_copy(i, j).wait_send()


def hand_over(unit_in, route_in, unit_ref, route_ref):
    unit_ref[...] = unit_in[...]
    route_ref[...] = route_in[...]


def shards(tokens, cotangent, expert_ids, route_weights, gate_weight, up_weight, down_weight, delta):
    n, ndp = lax.axis_size("exp"), lax.axis_size("dp")
    rows, width = tokens.shape
    chosen = expert_ids.shape[1]
    cap = rows * chosen * 3 // (2 * n)
    total = n * cap
    ff = gate_weight.shape[2]
    half, pairs = ff // 2, n // 2
    part = half // ndp
    blocks = width // 256 if width % 256 == 0 else 1
    unit = width // blocks
    cuts = (0, 2, 4, 6, 7) if blocks == 7 else (0, blocks)
    edges = tuple(c * unit for c in cuts)
    nc = len(edges) - 1
    ids = expert_ids.T
    shares = route_weights.T
    dma = pltpu.SemaphoreType.DMA
    hidden, ups, dots = pl.pallas_call(
        functools.partial(exchange_kernel, n, ndp, edges, cap),
        out_shape=(
            jax.ShapeDtypeStruct((pairs, 2 * cap, ff), BF16),
            jax.ShapeDtypeStruct((n, cap, width), BF16),
            jax.ShapeDtypeStruct((n, 1, rows), F32),
        ),
        in_specs=[VMEM, VMEM, VMEM, VMEM, HBM, HBM, HBM],
        out_specs=(VMEM, VMEM, VMEM),
        scratch_shapes=[
            pltpu.VMEM((width, ff), BF16),
            pltpu.VMEM((width, ff), BF16),
            pltpu.VMEM((ff, width), BF16),
            pltpu.VMEM((n, n, 8, rows), F32),
            pltpu.VMEM((2, n, rows, width), BF16),
            pltpu.VMEM((2, n, cap, width), BF16),
            pltpu.VMEM((2, n, cap, width), BF16),
            pltpu.VMEM((pairs, 2, 2 * cap, half), BF16),
            pltpu.VMEM((pairs, 2, 2 * cap, half), BF16),
            pltpu.VMEM((pairs, 2, 2 * cap, half), BF16),
            pltpu.VMEM((pairs, ndp, 2, 2 * cap, part), BF16),
            pltpu.VMEM((pairs, ndp, 2, 2 * cap, part), BF16),
            pltpu.VMEM((pairs, 2, 2 * cap, part), F32),
            pltpu.VMEM((pairs, 2, ndp, 2 * cap, part), BF16),
            dma((3,)), dma((n,)), dma((n,)),
            dma((2, pairs, nc)), dma((2, n, nc)), dma((2, n, nc)), dma((2, n, nc)),
            dma((pairs,)), dma((pairs,)),
            dma((pairs, ndp)), dma((pairs, ndp)),
            dma((pairs, ndp)), dma((pairs, ndp)),
            dma((pairs, ndp)), dma((pairs, ndp)),
        ],
        compiler_params=pltpu.CompilerParams(
            collective_id=0, has_side_effects=True, vmem_limit_bytes=60 * 2**20),
        name="exchange",
    )(ids, shares, tokens, cotangent, gate_weight, up_weight, down_weight)

    tile = 512
    chunks = ff // 128
    grad, sal = pl.pallas_call(
        functools.partial(gradient_kernel, tile),
        grid=(ff // tile,),
        out_shape=(
            jax.ShapeDtypeStruct((1, ff, width), F32),
            jax.ShapeDtypeStruct((chunks, 1, 128), F32),
        ),
        in_specs=[
            pl.BlockSpec((total, tile), lambda i: (0, i)),
            pl.BlockSpec((total, width), lambda i: (0, 0)),
            pl.BlockSpec((1, tile, width), lambda i: (0, i, 0)),
        ],
        out_specs=(
            pl.BlockSpec((1, tile, width), lambda i: (0, i, 0)),
            pl.BlockSpec((tile // 128, 1, 128), lambda i: (i, 0, 0)),
        ),
        compiler_params=pltpu.CompilerParams(vmem_limit_bytes=56 * 2**20),
        name="gradient",
    )(hidden.reshape(total, ff), ups.reshape(total, width), delta)

    peers = 2 * ndp
    units = chunks // peers
    unit, route = pl.pallas_call(
        functools.partial(reduce_kernel, n, ndp, float(width * peers)),
        out_shape=(
            jax.ShapeDtypeStruct((units, 1, 128), F32),
            jax.ShapeDtypeStruct((chosen, rows), F32),
        ),
        in_specs=[VMEM, VMEM, VMEM],
        out_specs=(VMEM, VMEM),
        scratch_shapes=[
            pltpu.VMEM((n, peers, 1, 128), F32),
            pltpu.VMEM((peers, units, 1, 128), F32),
            dma((n, peers)), dma((n, peers)), dma((peers,)), dma((peers,)),
        ],
        compiler_params=pltpu.CompilerParams(collective_id=1, has_side_effects=True),
        name="reduce",
    )(dots, sal, ids)
    unit, route = pl.pallas_call(
        hand_over,
        out_shape=(
            jax.ShapeDtypeStruct(unit.shape, F32),
            jax.ShapeDtypeStruct(route.shape, F32),
        ),
        in_specs=[VMEM, VMEM],
        out_specs=(VMEM, VMEM),
        name="hand_over",
    )(unit, route)
    return grad, unit.reshape(1, units * 128), route.T


def solution(mesh):
    return jax.shard_map(
        shards,
        mesh=mesh,
        in_specs=(
            P(("grp", "exp"), ("dp", "tp")),
            P(("grp", "exp"), ("dp", "tp")),
            P(("grp", "exp"), None),
            P(("grp", "exp"), None),
            P(("grp", "exp"), ("dp", "tp"), None),
            P(("grp", "exp"), ("dp", "tp"), None),
            P(("grp", "exp"), None, ("dp", "tp")),
            P(("grp", "exp"), None, ("dp", "tp")),
        ),
        out_specs=(
            P(("grp", "exp"), None, ("dp", "tp")),
            P(("grp", "exp"), ("dp", "tp")),
            P(("grp", "exp"), None),
        ),
        check_vma=False,
    )
```
